32 devices in a mesh: groups: 2 (over x), wide: 16 (over z, y, core).
Axes of the slice: x: 2, y: 2, z: 4, core: 2. Of those that a mesh axis runs over, the one named last changes fastest.
Arguments:
- sources: bfloat16 [64, 65536], P('groups', 'wide'), parts along dimension 0, may hold values from -6 to 6
- near_blocks: bfloat16 [3072, 256, 256], P(('groups', 'wide')), parts along dimension 0, may hold values from -0.375 to 0.375
- scale_table: float32 [1536], P('groups'), parts along dimension 0, may hold values from 0.25 to 1
- scale_index: int32 [3072], P(('groups', 'wide')), parts along dimension 0, may hold values from 0 to 767
- near_source: int32 [3072], P(('groups', 'wide')), parts along dimension 0, may hold values from 0 to 15
- near_target: int32 [3072], P(('groups', 'wide')), parts along dimension 0, may hold values from 0 to 255, as said below
- basis_in: bfloat16 [512, 64, 256], P(('groups', 'wide')), parts along dimension 0, may hold values from -0.375 to 0.375
- basis_out: bfloat16 [512, 64, 256], P(('groups', 'wide')), parts along dimension 0, may hold values from -0.1875 to 0.1875
- couplings: bfloat16 [8192, 64, 64], P(('groups', 'wide')), parts along dimension 0, may hold values from -0.75 to 0.75
- far_source: int32 [8192], P(('groups', 'wide')), parts along dimension 0, may hold values from 0 to 255
- far_target: int32 [8192], P(('groups', 'wide')), parts along dimension 0, may hold values from 0 to 15
Outputs:
- potentials: bfloat16 [64, 65536], P('groups', 'wide'), parts along dimension 0
The draws below stay inside these ranges and needn't reach their ends.
There are 2 independent parts, one for each index of `groups`. The reference program is written for one: setup_inputs(seed, part) draws one part's arguments, and reference() takes and returns one part's arrays. A program takes and returns all parts, laid end to end along the dimension named above; each array names one. Nothing has to cross between parts.
Inputs may be any that keep to these rules, and one draw needn't show every extreme that they name: `near_target`: in each aligned block of 96 entries (the pairs of one device), at most 6 entries name clusters of one owner (owner = cluster // 16), and some owner is named exactly 6 times in every block.
All inputs are finite; a program needn't handle non-finite values.
Results may differ from the reference program's by a relative error of at most 0.0054.
Values may be sent and summed in bfloat16 or wider, within the bound.
A program may use at most 128 MiB of HBM per device.

```python
import math
import jax
import jax.numpy as jnp
from jax import lax

BS = 256
RHS = 32
RANK = 64
CAP = 6
CL_DEV = 16
PAIR_DEV = 96
FAR_DEV = 256
CLUSTERS = 256
PANELS = 65536
PAIRS = 1536
FARS = 4096
SCALES = 768
N_WIDE = 16


def draw_near_target(key, part):
    key = jax.random.fold_in(key, 11)
    pop_key, pick_key = jax.random.split(key)
    grid_cells = N_WIDE * CAP
    demand_level = jax.random.randint(pop_key, (N_WIDE,), 0, 4)
    cell_index_list = jnp.arange(grid_cells, dtype=jnp.int32)
    cell_destination = cell_index_list // CAP

    def one_device(dkey):
        noise_key, full_key, local_key, mix_key = jax.random.split(dkey, 4)
        random_jitter = jax.random.randint(noise_key, (grid_cells,), 0, 2048)
        complete_destination = jax.random.randint(full_key, (), 0, N_WIDE)
        extra_reward = jnp.where(cell_destination == complete_destination, 8192, 0)
        ranking_value = (demand_level[cell_destination] * 1024 + random_jitter + extra_reward) * grid_cells + cell_index_list
        _, chosen = lax.top_k(ranking_value, PAIR_DEV)
        chosen = jax.random.permutation(mix_key, chosen)
        local = jax.random.randint(local_key, (PAIR_DEV,), 0, CL_DEV)
        return (chosen // CAP * CL_DEV + local).astype(jnp.int32)
    device_keys = jax.random.split(pick_key, N_WIDE)
    return jax.vmap(one_device)(device_keys).reshape(PAIRS)


def place_ends(array, rng, least, high):
    longest = array.shape.index(max(array.shape))
    spots = []
    for shift in (0, 1):
        where = [jax.random.randint(jax.random.fold_in(rng, axis), (), 0, length) for axis, length in enumerate(array.shape)]
        where[longest] = (where[longest] + shift) % array.shape[longest]
        spots.append(tuple(where))
    return array.at[spots[0]].set(least).at[spots[1]].set(high)


def shard_levels(rng, shape, pieces, low, largest):
    loudness = 1.0
    for axis_at, shards_of in pieces:
        heights = jax.random.uniform(jax.random.fold_in(jax.random.fold_in(rng, 6), axis_at), (shards_of,), jnp.float32, low / len(pieces), largest / len(pieces))
        loudness = loudness * jnp.repeat(jnp.exp(heights), shape[axis_at] // shards_of).reshape((-1,) + (1,) * (len(shape) - 1 - axis_at))
    return loudness


def normal_values(key, shape, deviation, limit, pieces=(), kind=jnp.bfloat16):
    drawn = deviation * jax.random.normal(key, shape, jnp.float32)
    if pieces:
        drawn = drawn * shard_levels(key, shape, pieces, -0.22, 0.18)
    return jnp.clip(drawn, -limit, limit).astype(kind)


def setup_inputs(seed: int = 0, part: int = 0) -> dict:
    streams_of = jax.random.split(jax.random.key(seed), 12)
    part_keys = jax.random.split(jax.random.fold_in(streams_of[11], part), 12)
    return {
        "sources": normal_values(part_keys[0], (RHS, PANELS), 1.0, 6.0, ((1, 16),)),
        "near_blocks": normal_values(part_keys[1], (PAIRS, BS, BS), BS ** -0.5, 0.375, ((0, 16),)),
        "scale_table": jnp.clip(jnp.exp(jax.random.uniform(part_keys[2], (SCALES,), jnp.float32, math.log(0.25), math.log(1.0))), 0.25, 1.0),
        "scale_index": place_ends(jax.random.randint(part_keys[3], (PAIRS,), 0, SCALES), jax.random.fold_in(part_keys[3], 1), 0, SCALES - 1).astype(jnp.int32),
        "near_source": place_ends(jax.random.randint(part_keys[4], (PAIRS,), 0, CL_DEV), jax.random.fold_in(part_keys[4], 1), 0, CL_DEV - 1).astype(jnp.int32),
        "near_target": draw_near_target(jax.random.fold_in(jax.random.fold_in(streams_of[11], part), 71), part),
        "basis_in": normal_values(part_keys[6], (CLUSTERS, RANK, BS), BS ** -0.5, 0.375, ((0, 16),)),
        "basis_out": normal_values(part_keys[7], (CLUSTERS, RANK, BS), (RANK * FAR_DEV // CL_DEV) ** -0.5, 0.1875, ((0, 16),)),
        "couplings": normal_values(part_keys[8], (FARS, RANK, RANK), RANK ** -0.5, 0.75, ((0, 16),)),
        "far_source": place_ends(jax.random.randint(part_keys[9], (FARS,), 0, CLUSTERS), jax.random.fold_in(part_keys[9], 1), 0, CLUSTERS - 1).astype(jnp.int32),
        "far_target": place_ends(jax.random.randint(part_keys[10], (FARS,), 0, CL_DEV), jax.random.fold_in(part_keys[10], 1), 0, CL_DEV - 1).astype(jnp.int32),
    }


def reference(sources, near_blocks, scale_table, scale_index, near_source, near_target, basis_in, basis_out, couplings, far_source, far_target):
    x_three = sources.reshape(RHS, CLUSTERS, BS)
    factor = scale_table[scale_index]
    owner_ids = jnp.arange(PAIRS, dtype=jnp.int32) // PAIR_DEV
    global_source = owner_ids * CL_DEV + near_source
    blocks_split = near_blocks.reshape(N_WIDE, PAIR_DEV, BS, BS)
    source_split = global_source.reshape(N_WIDE, PAIR_DEV)
    target_split = near_target.reshape(N_WIDE, PAIR_DEV)
    factor_split = factor.reshape(N_WIDE, PAIR_DEV)

    def one_owner(total, items):
        blocks, src, tgt, fac = items
        picked = jnp.take(x_three, src, axis=1).astype(jnp.float32)
        prods = jnp.einsum("rps,pts->prt", picked, blocks.astype(jnp.float32)) * fac[:, None, None]
        partial_sum = jnp.zeros((CLUSTERS, RHS, BS), jnp.float32).at[tgt].add(prods).astype(jnp.bfloat16)
        partial_sum = lax.optimization_barrier(partial_sum)
        return total + partial_sum.astype(jnp.float32), None

    near_field, _ = lax.scan(one_owner, jnp.zeros((CLUSTERS, RHS, BS), jnp.float32),
                             (blocks_split, source_split, target_split, factor_split))
    skeleton = jnp.einsum("rcs,cks->crk", x_three.astype(jnp.float32), basis_in.astype(jnp.float32)).astype(jnp.bfloat16)
    chosen = jnp.take(skeleton, far_source, axis=0).astype(jnp.float32)
    coupled = jnp.einsum("frk,fkm->frm", chosen, couplings.astype(jnp.float32))
    far_owner = jnp.arange(FARS, dtype=jnp.int32) // FAR_DEV
    global_target = far_owner * CL_DEV + far_target
    combined = jnp.zeros((CLUSTERS, RHS, RANK), jnp.float32).at[global_target].add(coupled).astype(jnp.bfloat16)
    far_field = jnp.einsum("crk,cks->crs", combined.astype(jnp.float32), basis_out.astype(jnp.float32))
    total = (near_field + far_field).astype(jnp.bfloat16)
    return jnp.transpose(total, (1, 0, 2)).reshape(RHS, PANELS)
```

```python
import functools

import jax
import jax.numpy as jnp
from jax import lax
from jax.experimental import pallas as pl
from jax.experimental.pallas import tpu as pltpu
from jax.sharding import PartitionSpec as P

CAP = 6
VMEM_LIMIT = 56 * 1024 * 1024
SMEM = pl.BlockSpec(memory_space=pltpu.SMEM)
VMEM = pl.BlockSpec(memory_space=pltpu.VMEM)
TRANSPOSED = (((1,), (1,)), ((), ()))
PLAIN = (((1,), (0,)), ((), ()))


def dot(a, b, dims=PLAIN):
    return lax.dot_general(a, b, dims, preferred_element_type=jnp.float32)


def prep_kernel(owners, target_ref, x_ref, basis_ref, skeleton_ref, slot_ref, code_ref, count_ref):
    clusters, rank, block = basis_ref.shape
    for o in range(owners):
        count_ref[o] = 0
    if code_ref.shape[0] != target_ref.shape[0]:
        @pl.loop(0, code_ref.shape[0])
        def _(j):
            code_ref[j] = -1

    @pl.loop(0, target_ref.shape[0])
    def _(p):
        t = target_ref[p]
        o = lax.div(t, clusters)
        c = count_ref[o]
        s = o * CAP + c
        slot_ref[p] = s
        code_ref[s] = t - o * clusters
        count_ref[o] = c + 1

    for c in range(0, clusters, 2):
        parts = [
            dot(x_ref[:, (c + i) * block:(c + i + 1) * block], basis_ref[c + i], TRANSPOSED)
            for i in range(2)
        ]
        skeleton_ref[:, c * rank:(c + 2) * rank] = jnp.concatenate(parts, axis=1).astype(
            jnp.bfloat16
        )


def near_kernel(
    pairs, slots, slot_ref, source_ref, index_ref, table_ref, x_ref, blocks_ref, out_ref
):
    step = pl.program_id(0)
    chunk, block, _ = blocks_ref.shape
    if slots != pairs:
        @pl.when(step == 0)
        def _():
            out_ref[...] = jnp.zeros_like(out_ref)

    for k in range(chunk):
        p = step * chunk + k
        xs = x_ref[:, pl.ds(pl.multiple_of(source_ref[p] * block, block), block)]
        product = dot(xs, blocks_ref[k], TRANSPOSED) * table_ref[index_ref[p]]
        out_ref[slot_ref[p]] = product.astype(jnp.bfloat16)


def far_kernel(source_ref, target_ref, skeleton_ref, couplings_ref, basis_ref, out_ref, acc_ref):
    step = pl.program_id(0)
    chunk, rank, _ = couplings_ref.shape
    clusters, _, block = basis_ref.shape
    rhs = skeleton_ref.shape[1]

    @pl.when(step == 0)
    def _():
        acc_ref[...] = jnp.zeros_like(acc_ref)

    half_of_lane = lax.broadcasted_iota(jnp.int32, (rhs, 2 * rank), 1) // rank
    group = 8
    for start in range(0, chunk, group):
        results = []
        for k in range(start, start + group):
            g = source_ref[step * chunk + k]
            owner = lax.div(g, clusters)
            inner = g - owner * clusters
            pair = lax.div(inner, 2)
            lanes = pl.ds(pl.multiple_of(pair * (2 * rank), 2 * rank), 2 * rank)
            both = skeleton_ref[owner, :, lanes]
            chosen = jnp.where(half_of_lane == inner - 2 * pair, both, jnp.zeros_like(both))
            coupling = couplings_ref[k]
            results.append(dot(chosen, jnp.concatenate([coupling, coupling], axis=0)))
        for k in range(group):
            t = target_ref[step * chunk + start + k]
            acc_ref[t] += results[k]

    @pl.when(step == pl.num_programs(0) - 1)
    def _():
        for c in range(clusters):
            out_ref[:, c * block:(c + 1) * block] = dot(
                acc_ref[c].astype(jnp.bfloat16), basis_ref[c]
            )


def final_kernel(owners, slots, code_ref, arrived_ref, far_ref, out_ref, acc_ref):
    block = arrived_ref.shape[2]
    me = lax.axis_index("wide")
    acc_ref[...] = far_ref[...]
    for d in range(owners):
        for k in range(CAP):
            c = jnp.maximum(code_ref[d * slots + me * CAP + k], 0)
            lanes = pl.ds(pl.multiple_of(c * block, block), block)
            acc_ref[:, lanes] += arrived_ref[d * CAP + k].astype(jnp.float32)
    out_ref[...] = acc_ref[...].astype(jnp.bfloat16)


def shards(
    sources,
    near_blocks,
    scale_table,
    scale_index,
    near_source,
    near_target,
    basis_in,
    basis_out,
    couplings,
    far_source,
    far_target,
):
    owners = lax.axis_size("wide")
    clusters, rank, block = basis_in.shape
    rhs = sources.shape[0]
    pairs = near_blocks.shape[0]
    fars = couplings.shape[0]
    slots = owners * CAP
    params = functools.partial(pltpu.CompilerParams, vmem_limit_bytes=VMEM_LIMIT)

    skeleton, slot, code = pl.pallas_call(
        functools.partial(prep_kernel, owners),
        out_shape=(
            jax.ShapeDtypeStruct((rhs, clusters * rank), jnp.bfloat16),
            jax.ShapeDtypeStruct((pairs,), jnp.int32),
            jax.ShapeDtypeStruct((slots,), jnp.int32),
        ),
        in_specs=[SMEM, VMEM, VMEM],
        out_specs=(VMEM, SMEM, SMEM),
        scratch_shapes=[pltpu.SMEM((owners,), jnp.int32)],
        compiler_params=params(),
        cost_estimate=pl.CostEstimate(
            flops=2 * rhs * rank * block * clusters, bytes_accessed=2 ** 20, transcendentals=0
        ),
    )(near_target, sources, basis_in)
    every = lax.all_gather(skeleton, "wide", axis=0, tiled=False)
    codes = lax.all_gather(code, "wide", axis=0, tiled=True)

    chunk = 12
    products = pl.pallas_call(
        functools.partial(near_kernel, pairs, slots),
        grid=(pairs // chunk,),
        out_shape=jax.ShapeDtypeStruct((slots, rhs, block), jnp.bfloat16),
        in_specs=[SMEM, SMEM, SMEM, SMEM, VMEM,
                  pl.BlockSpec((chunk, block, block), lambda i: (i, 0, 0))],
        out_specs=pl.BlockSpec((slots, rhs, block), lambda i: (0, 0, 0)),
        compiler_params=params(),
        cost_estimate=pl.CostEstimate(
            flops=2 * rhs * block * block * pairs,
            bytes_accessed=2 * pairs * block * block,
            transcendentals=0,
        ),
    )(slot, near_source, scale_index, scale_table, sources, near_blocks)
    arrived = lax.all_to_all(products, "wide", split_axis=0, concat_axis=0, tiled=True)

    far_chunk = 32
    far = pl.pallas_call(
        far_kernel,
        grid=(fars // far_chunk,),
        out_shape=jax.ShapeDtypeStruct((rhs, clusters * block), jnp.float32),
        in_specs=[SMEM, SMEM, VMEM,
                  pl.BlockSpec((far_chunk, rank, rank), lambda i: (i, 0, 0)), VMEM],
        out_specs=pl.BlockSpec((rhs, clusters * block), lambda i: (0, 0)),
        scratch_shapes=[pltpu.VMEM((clusters, rhs, rank), jnp.float32)],
        compiler_params=params(),
        cost_estimate=pl.CostEstimate(
            flops=2 * rhs * rank * (rank * fars + block * clusters),
            bytes_accessed=4 * fars * rank * rank + 2 ** 21,
            transcendentals=0,
        ),
    )(far_source, far_target, every, couplings, basis_out)

    return pl.pallas_call(
        functools.partial(final_kernel, owners, slots),
        out_shape=jax.ShapeDtypeStruct((rhs, clusters * block), jnp.bfloat16),
        in_specs=[SMEM, VMEM, VMEM],
        out_specs=VMEM,
        scratch_shapes=[pltpu.VMEM((rhs, clusters * block), jnp.float32)],
        compiler_params=params(),
    )(codes, arrived, far)


def solution(mesh):
    in_specs = (
        P("groups", "wide"),
        P(("groups", "wide"), None, None),
        P("groups"),
        P(("groups", "wide")),
        P(("groups", "wide")),
        P(("groups", "wide")),
        P(("groups", "wide"), None, None),
        P(("groups", "wide"), None, None),
        P(("groups", "wide"), None, None),
        P(("groups", "wide")),
        P(("groups", "wide")),
    )
    out_specs = P("groups", "wide")
    return jax.shard_map(shards, mesh=mesh, in_specs=in_specs, out_specs=out_specs, check_vma=False)
```

```python
import functools

import jax
import jax.numpy as jnp
from jax import lax
from jax.experimental import pallas as pl
from jax.experimental.pallas import tpu as pltpu
from jax.sharding import PartitionSpec as P

CAP = 6
TAIL = 16
VMEM_LIMIT = 56 * 1024 * 1024
SMEM = pl.BlockSpec(memory_space=pltpu.SMEM)
VMEM = pl.BlockSpec(memory_space=pltpu.VMEM)
TRANSPOSED = (((1,), (1,)), ((), ()))
PLAIN = (((1,), (0,)), ((), ()))


def dot(a, b, dims=PLAIN):
    return lax.dot_general(a, b, dims, preferred_element_type=jnp.float32)


def prep_kernel(
    owners, target_ref, index_ref, table_ref, x_ref, basis_ref,
    skeleton_ref, by_cluster_ref, perm_ref, code_ref, factor_ref, count_ref,
):
    clusters, rank, block = basis_ref.shape
    for o in range(owners):
        count_ref[o] = 0
    if code_ref.shape[0] != target_ref.shape[0]:
        @pl.loop(0, code_ref.shape[0])
        def _(j):
            code_ref[j] = 0
            perm_ref[j] = target_ref.shape[0]

    @pl.loop(0, target_ref.shape[0])
    def _(p):
        t = target_ref[p]
        o = lax.div(t, clusters)
        c = count_ref[o]
        s = o * CAP + c
        perm_ref[s] = p
        factor_ref[p] = table_ref[index_ref[p]]
        code_ref[s] = t - o * clusters
        count_ref[o] = c + 1

    for c in range(clusters):
        by_cluster_ref[c] = x_ref[:, c * block:(c + 1) * block]
    for c in range(0, clusters, 2):
        parts = [
            dot(x_ref[:, (c + i) * block:(c + i + 1) * block], basis_ref[c + i], TRANSPOSED)
            for i in range(2)
        ]
        skeleton_ref[:, c * rank:(c + 2) * rank] = jnp.concatenate(parts, axis=1).astype(
            jnp.bfloat16
        )


def flip(index, stride):
    return index + stride * (1 - 2 * lax.rem(lax.div(index, stride), 2))


def near_kernel(
    owners, perm_ref, code_ref, source_ref, factor_ref, skeleton_ref, x_ref, blocks_ref,
    out_ref, every_ref, held, products, load_sem, send_sem, recv_sem,
):
    chunks = load_sem.shape[0]
    pairs, block, _ = blocks_ref.shape
    chunk = pairs // chunks
    rhs = x_ref.shape[1]
    me = lax.axis_index("wide")
    strides = []
    stride = owners // 2
    while stride:
        strides.append(stride)
        stride //= 2

    def load(c):
        part = pl.ds(c * chunk, chunk)
        return pltpu.make_async_copy(blocks_ref.at[part], held.at[part], load_sem.at[c])

    for c in range(chunks):
        load(c).start()
    every_ref[me] = skeleton_ref[...]
    products[pairs] = jnp.zeros((rhs, block), jnp.bfloat16)
    barrier = pltpu.get_barrier_semaphore()
    for stride in strides:
        pl.semaphore_signal(
            barrier, inc=1, device_id={"wide": flip(me, stride)}, device_id_type=pl.DeviceIdType.MESH
        )
    pl.semaphore_wait(barrier, len(strides))

    have = [(0, me)]
    for n, stride in enumerate(strides):
        copies = []
        for offset, owner in have:
            copy = pltpu.make_async_remote_copy(
                src_ref=every_ref.at[owner],
                dst_ref=every_ref.at[owner],
                send_sem=send_sem.at[offset + stride],
                recv_sem=recv_sem.at[offset + stride],
                device_id={"wide": flip(me, stride)},
                device_id_type=pl.DeviceIdType.MESH,
            )
            copy.start()
            copies.append(copy)

        @pl.loop(n * chunks // len(strides), (n + 1) * chunks // len(strides))
        def _(c):
            load(c).wait()
            for k in range(chunk):
                p = c * chunk + k
                xs = x_ref[source_ref[p]]
                product = dot(xs, held[p], TRANSPOSED) * factor_ref[p]
                products[p] = product.astype(jnp.bfloat16)

        for copy in copies:
            copy.wait()
        have = have + [(offset + stride, flip(owner, stride)) for offset, owner in have]

    row = lax.broadcasted_iota(jnp.int32, (TAIL, block), 0)

    @pl.loop(0, owners)
    def _(o):
        tail = jnp.zeros((TAIL, block), jnp.float32)
        for k in range(CAP):
            j = o * CAP + k
            out_ref[o, k * rhs:(k + 1) * rhs, :] = products[perm_ref[j]]
            tail = jnp.where(row == k, code_ref[j].astype(jnp.float32), tail)
        out_ref[o, CAP * rhs:, :] = tail.astype(jnp.bfloat16)


def far_kernel(source_ref, target_ref, skeleton_ref, couplings_ref, basis_ref, out_ref, acc_ref):
    step = pl.program_id(0)
    chunk, rank, _ = couplings_ref.shape
    clusters, _, block = basis_ref.shape
    rhs = skeleton_ref.shape[1]

    @pl.when(step == 0)
    def _():
        acc_ref[...] = jnp.zeros_like(acc_ref)

    half_of_lane = lax.broadcasted_iota(jnp.int32, (rhs, 2 * rank), 1) // rank
    group = 8
    for start in range(0, chunk, group):
        results = []
        for k in range(start, start + group):
            g = source_ref[step * chunk + k]
            owner = lax.div(g, clusters)
            inner = g - owner * clusters
            pair = lax.div(inner, 2)
            lanes = pl.ds(pl.multiple_of(pair * (2 * rank), 2 * rank), 2 * rank)
            both = skeleton_ref[owner, :, lanes]
            chosen = jnp.where(half_of_lane == inner - 2 * pair, both, jnp.zeros_like(both))
            coupling = couplings_ref[k]
            results.append(dot(chosen, jnp.concatenate([coupling, coupling], axis=0)))
        for k in range(group):
            t = target_ref[step * chunk + start + k]
            acc_ref[t] += results[k]

    @pl.when(step == pl.num_programs(0) - 1)
    def _():
        for c in range(clusters):
            out_ref[:, c * block:(c + 1) * block] = dot(
                acc_ref[c].astype(jnp.bfloat16), basis_ref[c]
            )


def final_kernel(code_ref, arrived_ref, far_ref, out_ref, acc_ref):
    owners, _, block = arrived_ref.shape
    rhs = out_ref.shape[0]
    acc_ref[...] = far_ref[...]
    for d in range(owners):
        for k in range(CAP):
            lanes = pl.ds(pl.multiple_of(code_ref[d * CAP + k] * block, block), block)
            acc_ref[:, lanes] += arrived_ref[d, k * rhs:(k + 1) * rhs, :].astype(jnp.float32)
    out_ref[...] = acc_ref[...].astype(jnp.bfloat16)


def shards(
    sources,
    near_blocks,
    scale_table,
    scale_index,
    near_source,
    near_target,
    basis_in,
    basis_out,
    couplings,
    far_source,
    far_target,
):
    owners = lax.axis_size("wide")
    clusters, rank, block = basis_in.shape
    rhs = sources.shape[0]
    pairs = near_blocks.shape[0]
    fars = couplings.shape[0]
    slots = owners * CAP
    params = functools.partial(pltpu.CompilerParams, vmem_limit_bytes=VMEM_LIMIT)

    skeleton, by_cluster, perm, code, factor = pl.pallas_call(
        functools.partial(prep_kernel, owners),
        out_shape=(
            jax.ShapeDtypeStruct((rhs, clusters * rank), jnp.bfloat16),
            jax.ShapeDtypeStruct((clusters, rhs, block), jnp.bfloat16),
            jax.ShapeDtypeStruct((slots,), jnp.int32),
            jax.ShapeDtypeStruct((slots,), jnp.int32),
            jax.ShapeDtypeStruct((pairs,), jnp.float32),
        ),
        in_specs=[SMEM, SMEM, SMEM, VMEM, VMEM],
        out_specs=(VMEM, VMEM, SMEM, SMEM, SMEM),
        scratch_shapes=[pltpu.SMEM((owners,), jnp.int32)],
        compiler_params=params(),
        cost_estimate=pl.CostEstimate(
            flops=2 * rhs * rank * block * clusters, bytes_accessed=2 ** 20, transcendentals=0
        ),
    )(near_target, scale_index, scale_table, sources, basis_in)
    chunks = 8
    height = CAP * rhs + TAIL
    outgoing, every = pl.pallas_call(
        functools.partial(near_kernel, owners),
        out_shape=(
            jax.ShapeDtypeStruct((owners, height, block), jnp.bfloat16),
            jax.ShapeDtypeStruct((owners, rhs, clusters * rank), jnp.bfloat16),
        ),
        in_specs=[SMEM] * 4 + [VMEM, VMEM, pl.BlockSpec(memory_space=pl.ANY)],
        out_specs=(VMEM, VMEM),
        scratch_shapes=[
            pltpu.VMEM((pairs, block, block), jnp.bfloat16),
            pltpu.VMEM((pairs + 1, rhs, block), jnp.bfloat16),
            pltpu.SemaphoreType.DMA((chunks,)),
            pltpu.SemaphoreType.DMA((owners,)),
            pltpu.SemaphoreType.DMA((owners,)),
        ],
        compiler_params=params(collective_id=0, has_side_effects=True),
        cost_estimate=pl.CostEstimate(
            flops=2 * rhs * block * block * pairs,
            bytes_accessed=2 * pairs * block * block,
            transcendentals=0,
        ),
    )(perm, code, near_source, factor, skeleton, by_cluster, near_blocks)
    arrived = lax.all_to_all(outgoing, "wide", split_axis=0, concat_axis=0, tiled=True)
    codes = arrived[:, CAP * rhs:CAP * rhs + CAP, 0].astype(jnp.int32).reshape(slots)

    far_chunk = 32
    far = pl.pallas_call(
        far_kernel,
        grid=(fars // far_chunk,),
        out_shape=jax.ShapeDtypeStruct((rhs, clusters * block), jnp.float32),
        in_specs=[SMEM, SMEM, VMEM,
                  pl.BlockSpec((far_chunk, rank, rank), lambda i: (i, 0, 0)), VMEM],
        out_specs=pl.BlockSpec((rhs, clusters * block), lambda i: (0, 0)),
        scratch_shapes=[pltpu.VMEM((clusters, rhs, rank), jnp.float32)],
        compiler_params=params(),
        cost_estimate=pl.CostEstimate(
            flops=2 * rhs * rank * (rank * fars + block * clusters),
            bytes_accessed=4 * fars * rank * rank + 2 ** 21,
            transcendentals=0,
        ),
    )(far_source, far_target, every, couplings, basis_out)

    return pl.pallas_call(
        final_kernel,
        out_shape=jax.ShapeDtypeStruct((rhs, clusters * block), jnp.bfloat16),
        in_specs=[SMEM, VMEM, VMEM],
        out_specs=VMEM,
        scratch_shapes=[pltpu.VMEM((rhs, clusters * block), jnp.float32)],
        compiler_params=params(),
    )(codes, arrived, far)


def solution(mesh):
    in_specs = (
        P("groups", "wide"),
        P(("groups", "wide"), None, None),
        P("groups"),
        P(("groups", "wide")),
        P(("groups", "wide")),
        P(("groups", "wide")),
        P(("groups", "wide"), None, None),
        P(("groups", "wide"), None, None),
        P(("groups", "wide"), None, None),
        P(("groups", "wide")),
        P(("groups", "wide")),
    )
    out_specs = P("groups", "wide")
    return jax.shard_map(shards, mesh=mesh, in_specs=in_specs, out_specs=out_specs, check_vma=False)
```

```python
import functools

import jax
import jax.numpy as jnp
from jax import lax
from jax.experimental import pallas as pl
from jax.experimental.pallas import tpu as pltpu
from jax.sharding import PartitionSpec as P

CAP = 6
TAIL = 16
VMEM_LIMIT = 56 * 1024 * 1024
SMEM = pl.BlockSpec(memory_space=pltpu.SMEM)
VMEM = pl.BlockSpec(memory_space=pltpu.VMEM)
TRANSPOSED = (((1,), (1,)), ((), ()))
PLAIN = (((1,), (0,)), ((), ()))


def dot(a, b, dims=PLAIN):
    return lax.dot_general(a, b, dims, preferred_element_type=jnp.float32)


def prep_kernel(owners, target_ref, x_ref, basis_ref, skeleton_ref, slot_ref, code_ref, count_ref):
    clusters, rank, block = basis_ref.shape
    for o in range(owners):
        count_ref[o] = 0
    if code_ref.shape[0] != target_ref.shape[0]:
        @pl.loop(0, code_ref.shape[0])
        def _(j):
            code_ref[j] = 0

    @pl.loop(0, target_ref.shape[0])
    def _(p):
        t = target_ref[p]
        o = lax.div(t, clusters)
        c = count_ref[o]
        s = o * CAP + c
        slot_ref[p] = s
        code_ref[s] = t - o * clusters
        count_ref[o] = c + 1

    for c in range(0, clusters, 2):
        parts = [
            dot(x_ref[:, (c + i) * block:(c + i + 1) * block], basis_ref[c + i], TRANSPOSED)
            for i in range(2)
        ]
        skeleton_ref[:, c * rank:(c + 2) * rank] = jnp.concatenate(parts, axis=1).astype(
            jnp.bfloat16
        )


def flip(index, stride):
    return index + stride * (1 - 2 * lax.rem(lax.div(index, stride), 2))


def gather_kernel(owners, skeleton_ref, after_ref, every_ref, send_sem, recv_sem):
    me = lax.axis_index("wide")
    strides = []
    stride = owners // 2
    while stride:
        strides.append(stride)
        stride //= 2
    every_ref[me] = skeleton_ref[...]
    barrier = pltpu.get_barrier_semaphore()
    for stride in strides:
        pl.semaphore_signal(
            barrier, inc=1, device_id={"wide": flip(me, stride)}, device_id_type=pl.DeviceIdType.MESH
        )
    pl.semaphore_wait(barrier, len(strides))

    def send(offset, owner, stride):
        copy = pltpu.make_async_remote_copy(
            src_ref=every_ref.at[owner],
            dst_ref=every_ref.at[owner],
            send_sem=send_sem.at[offset + stride],
            recv_sem=recv_sem.at[offset + stride],
            device_id={"wide": flip(me, stride)},
            device_id_type=pl.DeviceIdType.MESH,
        )
        copy.start()
        return copy

    have = [(0, me)]
    copies = [[send(0, me, stride)] for stride in strides]
    for n, stride in enumerate(strides):
        for offset, owner in have[1:]:
            copies[n].append(send(offset, owner, stride))
        for copy in copies[n]:
            copy.wait()
        have = have + [(offset + stride, flip(owner, stride)) for offset, owner in have]


def near_kernel(
    pairs, slot_ref, code_ref, source_ref, index_ref, table_ref, x_ref, blocks_ref, out_ref
):
    step = pl.program_id(0)
    chunk, block, _ = blocks_ref.shape
    owners = out_ref.shape[0]
    rhs = x_ref.shape[0]

    @pl.when(step == 0)
    def _():
        if owners * CAP != pairs:
            out_ref[...] = jnp.zeros_like(out_ref)
        row = lax.broadcasted_iota(jnp.int32, (TAIL, block), 0)

        @pl.loop(0, owners)
        def _(o):
            tail = jnp.zeros((TAIL, block), jnp.float32)
            for k in range(CAP):
                tail = jnp.where(row == k, code_ref[o * CAP + k].astype(jnp.float32), tail)
            out_ref[o, CAP * rhs:, :] = tail.astype(jnp.bfloat16)

    for k in range(chunk):
        p = step * chunk + k
        xs = x_ref[:, pl.ds(pl.multiple_of(source_ref[p] * block, block), block)]
        product = dot(xs, blocks_ref[k], TRANSPOSED) * table_ref[index_ref[p]]
        o = lax.div(slot_ref[p], CAP)
        rows = pl.ds(pl.multiple_of((slot_ref[p] - o * CAP) * rhs, rhs), rhs)
        out_ref[o, rows, :] = product.astype(jnp.bfloat16)


def far_kernel(source_ref, target_ref, skeleton_ref, couplings_ref, basis_ref, out_ref, acc_ref):
    step = pl.program_id(0)
    chunk, rank, _ = couplings_ref.shape
    clusters, _, block = basis_ref.shape
    rhs = skeleton_ref.shape[1]

    @pl.when(step == 0)
    def _():
        acc_ref[...] = jnp.zeros_like(acc_ref)

    half_of_lane = lax.broadcasted_iota(jnp.int32, (rhs, 2 * rank), 1) // rank
    group = 8
    for start in range(0, chunk, group):
        results = []
        for k in range(start, start + group):
            g = source_ref[step * chunk + k]
            owner = lax.div(g, clusters)
            inner = g - owner * clusters
            pair = lax.div(inner, 2)
            lanes = pl.ds(pl.multiple_of(pair * (2 * rank), 2 * rank), 2 * rank)
            both = skeleton_ref[owner, :, lanes]
            chosen = jnp.where(half_of_lane == inner - 2 * pair, both, jnp.zeros_like(both))
            coupling = couplings_ref[k]
            results.append(dot(chosen, jnp.concatenate([coupling, coupling], axis=0)))
        for k in range(group):
            t = target_ref[step * chunk + start + k]
            acc_ref[t] += results[k]

    @pl.when(step == pl.num_programs(0) - 1)
    def _():
        for c in range(clusters):
            out_ref[:, c * block:(c + 1) * block] = dot(
                acc_ref[c].astype(jnp.bfloat16), basis_ref[c]
            )


def final_kernel(code_ref, arrived_ref, far_ref, out_ref, acc_ref):
    owners, _, block = arrived_ref.shape
    rhs = out_ref.shape[0]
    acc_ref[...] = far_ref[...]
    for d in range(owners):
        for k in range(CAP):
            lanes = pl.ds(pl.multiple_of(code_ref[d * CAP + k] * block, block), block)
            acc_ref[:, lanes] += arrived_ref[d, k * rhs:(k + 1) * rhs, :].astype(jnp.float32)
    out_ref[...] = acc_ref[...].astype(jnp.bfloat16)


def shards(
    sources,
    near_blocks,
    scale_table,
    scale_index,
    near_source,
    near_target,
    basis_in,
    basis_out,
    couplings,
    far_source,
    far_target,
):
    owners = lax.axis_size("wide")
    clusters, rank, block = basis_in.shape
    rhs = sources.shape[0]
    pairs = near_blocks.shape[0]
    fars = couplings.shape[0]
    slots = owners * CAP
    params = functools.partial(pltpu.CompilerParams, vmem_limit_bytes=VMEM_LIMIT)

    skeleton, slot, code = pl.pallas_call(
        functools.partial(prep_kernel, owners),
        out_shape=(
            jax.ShapeDtypeStruct((rhs, clusters * rank), jnp.bfloat16),
            jax.ShapeDtypeStruct((pairs,), jnp.int32),
            jax.ShapeDtypeStruct((slots,), jnp.int32),
        ),
        in_specs=[SMEM, VMEM, VMEM],
        out_specs=(VMEM, SMEM, SMEM),
        scratch_shapes=[pltpu.SMEM((owners,), jnp.int32)],
        compiler_params=params(),
        cost_estimate=pl.CostEstimate(
            flops=2 * rhs * rank * block * clusters, bytes_accessed=2 ** 20, transcendentals=0
        ),
    )(near_target, sources, basis_in)
    chunk = 12
    height = CAP * rhs + TAIL
    outgoing = pl.pallas_call(
        functools.partial(near_kernel, pairs),
        grid=(pairs // chunk,),
        out_shape=jax.ShapeDtypeStruct((owners, height, block), jnp.bfloat16),
        in_specs=[SMEM, SMEM, SMEM, SMEM, SMEM, VMEM,
                  pl.BlockSpec((chunk, block, block), lambda i: (i, 0, 0))],
        out_specs=pl.BlockSpec((owners, height, block), lambda i: (0, 0, 0)),
        compiler_params=params(),
        cost_estimate=pl.CostEstimate(
            flops=2 * rhs * block * block * pairs,
            bytes_accessed=2 * pairs * block * block,
            transcendentals=0,
        ),
    )(slot, code, near_source, scale_index, scale_table, sources, near_blocks)
    arrived = lax.all_to_all(outgoing, "wide", split_axis=0, concat_axis=0, tiled=True)
    codes = arrived[:, CAP * rhs:CAP * rhs + CAP, 0].astype(jnp.int32).reshape(slots)
    every = pl.pallas_call(
        functools.partial(gather_kernel, owners),
        out_shape=jax.ShapeDtypeStruct((owners, rhs, clusters * rank), jnp.bfloat16),
        in_specs=[VMEM, pl.BlockSpec(memory_space=pl.ANY)],
        out_specs=VMEM,
        scratch_shapes=[
            pltpu.SemaphoreType.DMA((owners,)),
            pltpu.SemaphoreType.DMA((owners,)),
        ],
        compiler_params=params(collective_id=0, has_side_effects=True),
        cost_estimate=pl.CostEstimate(flops=0, bytes_accessed=2 ** 25, transcendentals=0),
    )(skeleton, outgoing)

    far_chunk = 32
    far = pl.pallas_call(
        far_kernel,
        grid=(fars // far_chunk,),
        out_shape=jax.ShapeDtypeStruct((rhs, clusters * block), jnp.float32),
        in_specs=[SMEM, SMEM, VMEM,
                  pl.BlockSpec((far_chunk, rank, rank), lambda i: (i, 0, 0)), VMEM],
        out_specs=pl.BlockSpec((rhs, clusters * block), lambda i: (0, 0)),
        scratch_shapes=[pltpu.VMEM((clusters, rhs, rank), jnp.float32)],
        compiler_params=params(),
        cost_estimate=pl.CostEstimate(
            flops=2 * rhs * rank * (rank * fars + block * clusters),
            bytes_accessed=4 * fars * rank * rank + 2 ** 21,
            transcendentals=0,
        ),
    )(far_source, far_target, every, couplings, basis_out)

    return pl.pallas_call(
        final_kernel,
        out_shape=jax.ShapeDtypeStruct((rhs, clusters * block), jnp.bfloat16),
        in_specs=[SMEM, VMEM, VMEM],
        out_specs=VMEM,
        scratch_shapes=[pltpu.VMEM((rhs, clusters * block), jnp.float32)],
        compiler_params=params(),
    )(codes, arrived, far)


def solution(mesh):
    in_specs = (
        P("groups", "wide"),
        P(("groups", "wide"), None, None),
        P("groups"),
        P(("groups", "wide")),
        P(("groups", "wide")),
        P(("groups", "wide")),
        P(("groups", "wide"), None, None),
        P(("groups", "wide"), None, None),
        P(("groups", "wide"), None, None),
        P(("groups", "wide")),
        P(("groups", "wide")),
    )
    out_specs = P("groups", "wide")
    return jax.shard_map(shards, mesh=mesh, in_specs=in_specs, out_specs=out_specs, check_vma=False)
```

```python
import functools

import jax
import jax.numpy as jnp
from jax import lax
from jax.experimental import pallas as pl
from jax.experimental.pallas import tpu as pltpu
from jax.sharding import PartitionSpec as P

CAP = 6
TAIL = 16
VMEM_LIMIT = 56 * 1024 * 1024
SMEM = pl.BlockSpec(memory_space=pltpu.SMEM)
VMEM = pl.BlockSpec(memory_space=pltpu.VMEM)
TRANSPOSED = (((1,), (1,)), ((), ()))
PLAIN = (((1,), (0,)), ((), ()))


def dot(a, b, dims=PLAIN):
    return lax.dot_general(a, b, dims, preferred_element_type=jnp.float32)


def prep_kernel(
    owners, target_ref, index_ref, table_ref, x_ref, basis_ref,
    skeleton_ref, by_cluster_ref, perm_ref, code_ref, factor_ref, count_ref,
):
    clusters, rank, block = basis_ref.shape
    for o in range(owners):
        count_ref[o] = 0
    if code_ref.shape[0] != target_ref.shape[0]:
        @pl.loop(0, code_ref.shape[0])
        def _(j):
            code_ref[j] = 0
            perm_ref[j] = target_ref.shape[0]

    @pl.loop(0, target_ref.shape[0])
    def _(p):
        t = target_ref[p]
        o = lax.div(t, clusters)
        c = count_ref[o]
        s = o * CAP + c
        perm_ref[s] = p
        factor_ref[p] = table_ref[index_ref[p]]
        code_ref[s] = t - o * clusters
        count_ref[o] = c + 1

    for c in range(clusters):
        by_cluster_ref[c] = x_ref[:, c * block:(c + 1) * block]
    for c in range(0, clusters, 2):
        parts = [
            dot(x_ref[:, (c + i) * block:(c + i + 1) * block], basis_ref[c + i], TRANSPOSED)
            for i in range(2)
        ]
        skeleton_ref[:, c * rank:(c + 2) * rank] = jnp.concatenate(parts, axis=1).astype(
            jnp.bfloat16
        )


def flip(index, stride):
    return index + stride * (1 - 2 * lax.rem(lax.div(index, stride), 2))


def near_kernel(
    owners, perm_ref, code_ref, source_ref, factor_ref, skeleton_ref, x_ref, blocks_ref,
    out_ref, every_ref, held, products, load_sem, send_sem, recv_sem,
):
    chunks = load_sem.shape[0]
    pairs, block, _ = blocks_ref.shape
    chunk = pairs // chunks
    rhs = x_ref.shape[1]
    me = lax.axis_index("wide")
    strides = []
    stride = owners // 2
    while stride:
        strides.append(stride)
        stride //= 2

    def load(c):
        part = pl.ds(c * chunk, chunk)
        return pltpu.make_async_copy(blocks_ref.at[part], held.at[part], load_sem.at[c])

    for c in range(chunks):
        load(c).start()
    every_ref[me] = skeleton_ref[...]
    products[pairs] = jnp.zeros((rhs, block), jnp.bfloat16)
    barrier = pltpu.get_barrier_semaphore()
    for stride in strides:
        pl.semaphore_signal(
            barrier, inc=1, device_id={"wide": flip(me, stride)}, device_id_type=pl.DeviceIdType.MESH
        )
    pl.semaphore_wait(barrier, len(strides))

    def send(offset, owner, stride):
        copy = pltpu.make_async_remote_copy(
            src_ref=every_ref.at[owner],
            dst_ref=every_ref.at[owner],
            send_sem=send_sem.at[offset + stride],
            recv_sem=recv_sem.at[offset + stride],
            device_id={"wide": flip(me, stride)},
            device_id_type=pl.DeviceIdType.MESH,
        )
        copy.start()
        return copy

    have = [(0, me)]
    waiting = [[send(0, me, stride)] for stride in strides]
    for n, stride in enumerate(strides):
        copies = waiting[n] + [send(offset, owner, stride) for offset, owner in have[1:]]

        @pl.loop(n * chunks // len(strides), (n + 1) * chunks // len(strides))
        def _(c):
            load(c).wait()
            for k in range(chunk):
                p = c * chunk + k
                xs = x_ref[source_ref[p]]
                product = dot(xs, held[p], TRANSPOSED) * factor_ref[p]
                products[p] = product.astype(jnp.bfloat16)

        for copy in copies:
            copy.wait()
        have = have + [(offset + stride, flip(owner, stride)) for offset, owner in have]

    row = lax.broadcasted_iota(jnp.int32, (TAIL, block), 0)

    @pl.loop(0, owners)
    def _(o):
        tail = jnp.zeros((TAIL, block), jnp.float32)
        for k in range(CAP):
            j = o * CAP + k
            out_ref[o, k * rhs:(k + 1) * rhs, :] = products[perm_ref[j]]
            tail = jnp.where(row == k, code_ref[j].astype(jnp.float32), tail)
        out_ref[o, CAP * rhs:, :] = tail.astype(jnp.bfloat16)


def far_kernel(source_ref, target_ref, skeleton_ref, couplings_ref, basis_ref, out_ref, acc_ref):
    step = pl.program_id(0)
    chunk, rank, _ = couplings_ref.shape
    clusters, _, block = basis_ref.shape
    rhs = skeleton_ref.shape[1]

    @pl.when(step == 0)
    def _():
        acc_ref[...] = jnp.zeros_like(acc_ref)

    half_of_lane = lax.broadcasted_iota(jnp.int32, (rhs, 2 * rank), 1) // rank
    group = 8
    for start in range(0, chunk, group):
        results = []
        for k in range(start, start + group):
            g = source_ref[step * chunk + k]
            owner = lax.div(g, clusters)
            inner = g - owner * clusters
            pair = lax.div(inner, 2)
            lanes = pl.ds(pl.multiple_of(pair * (2 * rank), 2 * rank), 2 * rank)
            both = skeleton_ref[owner, :, lanes]
            chosen = jnp.where(half_of_lane == inner - 2 * pair, both, jnp.zeros_like(both))
            coupling = couplings_ref[k]
            results.append(dot(chosen, jnp.concatenate([coupling, coupling], axis=0)))
        for k in range(group):
            t = target_ref[step * chunk + start + k]
            acc_ref[t] += results[k]

    @pl.when(step == pl.num_programs(0) - 1)
    def _():
        for c in range(clusters):
            out_ref[:, c * block:(c + 1) * block] = dot(
                acc_ref[c].astype(jnp.bfloat16), basis_ref[c]
            )


def final_kernel(code_ref, arrived_ref, far_ref, out_ref, acc_ref):
    owners, _, block = arrived_ref.shape
    rhs = out_ref.shape[0]
    acc_ref[...] = far_ref[...]
    for d in range(owners):
        for k in range(CAP):
            lanes = pl.ds(pl.multiple_of(code_ref[d * CAP + k] * block, block), block)
            acc_ref[:, lanes] += arrived_ref[d, k * rhs:(k + 1) * rhs, :].astype(jnp.float32)
    out_ref[...] = acc_ref[...].astype(jnp.bfloat16)


def shards(
    sources,
    near_blocks,
    scale_table,
    scale_index,
    near_source,
    near_target,
    basis_in,
    basis_out,
    couplings,
    far_source,
    far_target,
):
    owners = lax.axis_size("wide")
    clusters, rank, block = basis_in.shape
    rhs = sources.shape[0]
    pairs = near_blocks.shape[0]
    fars = couplings.shape[0]
    slots = owners * CAP
    params = functools.partial(pltpu.CompilerParams, vmem_limit_bytes=VMEM_LIMIT)

    skeleton, by_cluster, perm, code, factor = pl.pallas_call(
        functools.partial(prep_kernel, owners),
        out_shape=(
            jax.ShapeDtypeStruct((rhs, clusters * rank), jnp.bfloat16),
            jax.ShapeDtypeStruct((clusters, rhs, block), jnp.bfloat16),
            jax.ShapeDtypeStruct((slots,), jnp.int32),
            jax.ShapeDtypeStruct((slots,), jnp.int32),
            jax.ShapeDtypeStruct((pairs,), jnp.float32),
        ),
        in_specs=[SMEM, SMEM, SMEM, VMEM, VMEM],
        out_specs=(VMEM, VMEM, SMEM, SMEM, SMEM),
        scratch_shapes=[pltpu.SMEM((owners,), jnp.int32)],
        compiler_params=params(),
        cost_estimate=pl.CostEstimate(
            flops=2 * rhs * rank * block * clusters, bytes_accessed=2 ** 20, transcendentals=0
        ),
    )(near_target, scale_index, scale_table, sources, basis_in)
    chunks = 8
    height = CAP * rhs + TAIL
    outgoing, every = pl.pallas_call(
        functools.partial(near_kernel, owners),
        out_shape=(
            jax.ShapeDtypeStruct((owners, height, block), jnp.bfloat16),
            jax.ShapeDtypeStruct((owners, rhs, clusters * rank), jnp.bfloat16),
        ),
        in_specs=[SMEM] * 4 + [VMEM, VMEM, pl.BlockSpec(memory_space=pl.ANY)],
        out_specs=(VMEM, VMEM),
        scratch_shapes=[
            pltpu.VMEM((pairs, block, block), jnp.bfloat16),
            pltpu.VMEM((pairs + 1, rhs, block), jnp.bfloat16),
            pltpu.SemaphoreType.DMA((chunks,)),
            pltpu.SemaphoreType.DMA((owners,)),
            pltpu.SemaphoreType.DMA((owners,)),
        ],
        compiler_params=params(collective_id=0, has_side_effects=True),
        cost_estimate=pl.CostEstimate(
            flops=2 * rhs * block * block * pairs,
            bytes_accessed=2 * pairs * block * block,
            transcendentals=0,
        ),
    )(perm, code, near_source, factor, skeleton, by_cluster, near_blocks)
    arrived = lax.all_to_all(outgoing, "wide", split_axis=0, concat_axis=0, tiled=True)
    codes = arrived[:, CAP * rhs:CAP * rhs + CAP, 0].astype(jnp.int32).reshape(slots)

    far_chunk = 32
    far = pl.pallas_call(
        far_kernel,
        grid=(fars // far_chunk,),
        out_shape=jax.ShapeDtypeStruct((rhs, clusters * block), jnp.float32),
        in_specs=[SMEM, SMEM, VMEM,
                  pl.BlockSpec((far_chunk, rank, rank), lambda i: (i, 0, 0)), VMEM],
        out_specs=pl.BlockSpec((rhs, clusters * block), lambda i: (0, 0)),
        scratch_shapes=[pltpu.VMEM((clusters, rhs, rank), jnp.float32)],
        compiler_params=params(),
        cost_estimate=pl.CostEstimate(
            flops=2 * rhs * rank * (rank * fars + block * clusters),
            bytes_accessed=4 * fars * rank * rank + 2 ** 21,
            transcendentals=0,
        ),
    )(far_source, far_target, every, couplings, basis_out)

    return pl.pallas_call(
        final_kernel,
        out_shape=jax.ShapeDtypeStruct((rhs, clusters * block), jnp.bfloat16),
        in_specs=[SMEM, VMEM, VMEM],
        out_specs=VMEM,
        scratch_shapes=[pltpu.VMEM((rhs, clusters * block), jnp.float32)],
        compiler_params=params(),
    )(codes, arrived, far)


def solution(mesh):
    in_specs = (
        P("groups", "wide"),
        P(("groups", "wide"), None, None),
        P("groups"),
        P(("groups", "wide")),
        P(("groups", "wide")),
        P(("groups", "wide")),
        P(("groups", "wide"), None, None),
        P(("groups", "wide"), None, None),
        P(("groups", "wide"), None, None),
        P(("groups", "wide")),
        P(("groups", "wide")),
    )
    out_specs = P("groups", "wide")
    return jax.shard_map(shards, mesh=mesh, in_specs=in_specs, out_specs=out_specs, check_vma=False)
```
